32 devices in a mesh: grp: 2 (over y), leaf: 4 (over z), head: 4 (over x, core).
Axes of the slice: x: 2, y: 2, z: 4, core: 2. Of those that a mesh axis runs over, the one named last changes fastest.
Arguments:
- query: bfloat16 [2560, 8192], P(('grp', 'leaf'), 'head'), parts along dimension 0, may hold values from -100 to 100
- key_value: bfloat16 [2560, 2048], P(('grp', 'leaf'), 'head'), parts along dimension 0, may hold values from -4 to 4
- grad_out: bfloat16 [2560, 8192], P(('grp', 'leaf'), 'head'), parts along dimension 0, may hold values from -6 to 6
- lengths: int32 [40], P(('grp', 'leaf')), parts along dimension 0, may hold values from 1 to 64, 960 in all
- ancestors: int32 [40, 4], P(('grp', 'leaf')), parts along dimension 0, may hold values from -1 to 18, as said below
Outputs:
- grad_query: bfloat16 [2560, 8192], P(('grp', 'leaf'), 'head'), parts along dimension 0
- grad_key_value: bfloat16 [2560, 2048], P(('grp', 'leaf'), 'head'), parts along dimension 0
The draws below stay inside these ranges and needn't reach their ends.
There are 2 independent parts, one for each index of `grp`. The reference program is written for one: setup_inputs(seed, part) draws one part's arguments, and reference() takes and returns one part's arrays. A program takes and returns all parts, laid end to end along the dimension named above; each array names one. Nothing has to cross between parts.
Inputs may be any that keep to these rules, and one draw needn't show every extreme that they name: Segment g sits in slot g % 5 of leaf block g // 5. A segment in slot j lists its j ancestors, entry l being the ancestor in slot l (its chain from the root), and -1 in the other entries. `lengths`: the largest is 64 in every draw.
All inputs are finite; a program needn't handle non-finite values. No bound on the sum of `lengths` on one device may be relied on, other than what follows from the above.
Results may differ from the reference program's by a relative error of at most 0.0075.
Values may be sent and summed in bfloat16 or wider, within the bound.
A program may use at most 64 MiB of HBM per device.

```python
import math
import jax
import jax.numpy as jnp
import numpy as np
from jax import lax

QH = 64
KVH = 8
HD = 128
SLOT = 64
SEG_DEV = 5
SEGS = 20
TOKENS = 1280
N_LEAF = 4


def shared_keys(key):
    return jnp.clip(jax.random.normal(key, (TOKENS, KVH, HD), jnp.float32), -4.0, 4.0)


def draw_query(key, part):
    key = jax.random.fold_in(key, 1)
    first = jax.random.fold_in(key, 0)
    values = jnp.clip(jax.random.normal(first, (TOKENS, KVH, QH // KVH, HD), jnp.float32), -6.0, 6.0)
    return values.reshape(TOKENS, QH * HD).astype(jnp.bfloat16)


def draw_key_value(key, part):
    base = shared_keys(key)
    key = jax.random.fold_in(key, 2)
    values = jnp.clip(jax.random.normal(key, (TOKENS, KVH, HD), jnp.float32), -4.0, 4.0)
    return jnp.stack([base, values], 2).reshape(TOKENS, 2 * KVH * HD).astype(jnp.bfloat16)


def draw_ancestors(key, part):
    key = jax.random.fold_in(key, 3)
    levels = [jnp.full((N_LEAF, SEG_DEV - 1), -1, jnp.int32)]
    for level_index in range(1, SEG_DEV):
        key, first, second = jax.random.split(key, 3)
        pick_one = jax.random.randint(first, (N_LEAF,), 0, N_LEAF)
        pick_two = jax.random.randint(second, (N_LEAF,), 0, N_LEAF)
        parent_dev = jnp.minimum(pick_one, pick_two).at[0].set(N_LEAF - 1)
        parent_id = (parent_dev * SEG_DEV + level_index - 1).astype(jnp.int32)
        previous = levels[level_index - 1][parent_dev]
        levels.append(previous.at[:, level_index - 1].set(parent_id))
    return jnp.stack(levels, 1).reshape(SEGS, SEG_DEV - 1).astype(jnp.int32)


def block_scale(own_key, extent, shards, least, high):
    factor_of, own = 1.0, jax.random.fold_in(own_key, 6)
    for dim, blocks in shards:
        steps = jnp.exp(jax.random.uniform(jax.random.fold_in(own, dim), (blocks,), jnp.float32, least / len(shards), high / len(shards)))
        factor_of = factor_of * jnp.repeat(steps, extent[dim] // blocks).reshape([-1 if axis == dim else 1 for axis in range(len(extent))])
    return factor_of


def length_profile(number_of, total, reach, slope):
    portions = [(1 << 20) // math.isqrt(standing ** slope) + 1 for standing in range(2, number_of + 1)]
    rest, holding = total - reach - (number_of - 1), [1] * (number_of - 1)
    while rest > 0:
        movable = [i for i in range(number_of - 1) if holding[i] < reach]
        mass, remaining = sum([portions[i] for i in movable]), rest
        for i in movable:
            more = min(reach - holding[i], max(1, remaining * portions[i] // mass), rest)
            holding[i] = holding[i] + more
            rest = rest - more
    return np.array([reach] + holding)


def ragged_sizes(rng, count, total, reach, slope):
    if count == 2:
        one = jax.random.randint(rng, (), max(1, total - reach), min(reach, total - 1) + 1)
        return jnp.stack([one, total - one])
    tallies = jnp.asarray(length_profile(count, total, reach, slope), jnp.int32)
    twos = (count - 1) // 2
    donor, taker = tallies[1:1 + 2 * twos:2], tallies[2:2 + 2 * twos:2]
    room = jnp.minimum(donor - 1, reach - taker)
    passed = jax.random.randint(jax.random.fold_in(rng, 1), (twos,), 0, 1 << 20) % (room + 1)
    tallies = tallies.at[1:1 + 2 * twos:2].set(donor - passed).at[2:2 + 2 * twos:2].set(taker + passed)
    return tallies[jax.random.permutation(jax.random.fold_in(rng, 2), count)]


def gaussian(rng, extent, width, limit, cuts=(), kind=jnp.bfloat16):
    values = width * jax.random.normal(rng, extent, jnp.float32)
    if cuts:
        values = values * block_scale(rng, extent, cuts, -0.22, 0.18)
    return jnp.clip(values, -limit, limit).astype(kind)


def setup_inputs(seed: int = 0, part: int = 0) -> dict:
    key_list = jax.random.split(jax.random.key(seed), 6)
    part_keys = jax.random.split(jax.random.fold_in(key_list[5], part), 6)
    return {
        "query": draw_query(jax.random.fold_in(jax.random.fold_in(key_list[5], part), 71), part),
        "key_value": draw_key_value(jax.random.fold_in(jax.random.fold_in(key_list[5], part), 71), part),
        "grad_out": gaussian(part_keys[2], (TOKENS, QH * HD), 1.0, 6.0, ((0, 4), (1, 4))),
        "lengths": ragged_sizes(part_keys[3], SEGS, SEGS * SLOT * 3 // 4, SLOT, 0).astype(jnp.int32),
        "ancestors": draw_ancestors(jax.random.fold_in(jax.random.fold_in(key_list[5], part), 71), part),
    }


masked_score = -1e30


def rounded(values):
    return lax.optimization_barrier(values.astype(jnp.bfloat16)).astype(jnp.float32)


def attend(queries, cotangent, key_rows, allowed, inv_root):
    key_part = key_rows[:, 0]
    value_part = key_rows[:, 1]
    scores = jnp.einsum("qgd,td->gqt", queries, key_part) * inv_root
    scores = jnp.where(allowed[None], scores, masked_score)
    row_max = jnp.max(scores, -1, keepdims=True)
    exp_scores = jnp.exp(scores - row_max)
    softmax_w = exp_scores / jnp.sum(exp_scores, -1, keepdims=True)
    weights_b = rounded(softmax_w)
    recomputed = jnp.einsum("gqt,td->qgd", weights_b, value_part)
    row_delta = jnp.sum(cotangent * recomputed, -1)
    grad_weights = jnp.einsum("qgd,td->gqt", cotangent, value_part)
    grad_scores = rounded(softmax_w * (grad_weights - jnp.transpose(row_delta)[:, :, None]))
    grad_q = jnp.einsum("gqt,td->qgd", grad_scores, key_part) * inv_root
    grad_k = jnp.einsum("gqt,qgd->td", grad_scores, queries) * inv_root
    grad_v = jnp.einsum("gqt,qgd->td", weights_b, cotangent)
    return grad_q, jnp.stack([grad_k, grad_v], 1)


def head_grads(queries, key_values, cotangents, lengths, ancestors):
    inv_root = HD ** -0.5
    positions = jnp.arange(SLOT)

    def block_step(accumulated, block_index):
        partial_value = jnp.zeros((SEGS, SLOT, 2, HD), jnp.float32)
        grad_list = []
        own_list = []
        for slot_index in range(SEG_DEV):
            segment = block_index * SEG_DEV + slot_index
            row_valid = positions < lengths[segment]
            query_rows = queries[segment].astype(jnp.float32)
            cotangent = jnp.where(row_valid[:, None, None], cotangents[segment], jnp.zeros((), jnp.bfloat16)).astype(jnp.float32)
            pieces = []
            key_masks = []
            owners = []
            for level_index in range(slot_index):
                segment_id = ancestors[segment, level_index]
                pieces.append(key_values[segment_id].astype(jnp.float32))
                key_masks.append(jnp.broadcast_to(positions[None, :] < lengths[segment_id], (SLOT, SLOT)))
                owners.append(segment_id)
            pieces.append(key_values[segment].astype(jnp.float32))
            key_masks.append((positions[None, :] <= positions[:, None]) & row_valid[None, :])
            grad_q, grad_kv = attend(query_rows, cotangent, jnp.concatenate(pieces, 0), jnp.concatenate(key_masks, 1), inv_root)
            for level_index, segment_id in enumerate(owners):
                partial_value = partial_value.at[segment_id].add(grad_kv[level_index * SLOT:(level_index + 1) * SLOT])
            grad_list.append(grad_q)
            own_list.append(grad_kv[slot_index * SLOT:])
        accumulated = accumulated + rounded(partial_value)
        return accumulated, (jnp.stack(grad_list), jnp.stack(own_list))

    accumulated, (grad_q, own_terms) = lax.scan(block_step, jnp.zeros((SEGS, SLOT, 2, HD), jnp.float32), jnp.arange(N_LEAF))
    grad_q = grad_q.reshape(SEGS, SLOT, -1, HD)
    own_terms = own_terms.reshape(SEGS, SLOT, 2, HD)
    return grad_q.astype(jnp.bfloat16), (own_terms + accumulated).astype(jnp.bfloat16)


def reference(query, key_value, grad_out, lengths, ancestors):
    group_size = QH // KVH
    queries = query.reshape(SEGS, SLOT, KVH, group_size, HD).transpose(2, 0, 1, 3, 4)
    key_values = key_value.reshape(SEGS, SLOT, KVH, 2, HD).transpose(2, 0, 1, 3, 4)
    cotangents = grad_out.reshape(SEGS, SLOT, KVH, group_size, HD).transpose(2, 0, 1, 3, 4)

    def per_head(operands):
        return head_grads(operands[0], operands[1], operands[2], lengths, ancestors)

    grad_q, grad_kv = lax.map(per_head, (queries, key_values, cotangents))
    grad_query = grad_q.transpose(1, 2, 0, 3, 4).reshape(TOKENS, QH * HD)
    grad_key_value = grad_kv.transpose(1, 2, 0, 3, 4).reshape(TOKENS, 2 * KVH * HD)
    return grad_query, grad_key_value
```

```python
import functools
import math

import jax
import jax.numpy as jnp
from jax import lax
from jax.experimental import pallas as pl
from jax.experimental.pallas import tpu as pltpu
from jax.sharding import PartitionSpec as P

HD = 128
SLOT = 64
SEG_DEV = 5


masked_score = -1e30


def from_partner(block, axis, bit):
    count = lax.axis_size(axis)
    route = []
    for low in range(count):
        high = low | 1 << bit
        if high != low and high < count:
            route += [(low, high), (high, low)]
    return lax.ppermute(block, axis, route)


def as_sent(array):

    def short(part):
        return part.astype(jnp.bfloat16) if part.dtype == jnp.float32 else part

    return jax.tree.map(short, array)


def attend(queries, cotangent, key_rows, allowed, inv_root):
    key_part = key_rows[:, :, 0]
    value_part = key_rows[:, :, 1]
    scores = (
        jnp.einsum("qkgd,tkd->kgqt", queries, key_part, preferred_element_type=jnp.float32)
        * inv_root
    )
    scores = jnp.where(allowed, scores, masked_score)
    row_max = jnp.max(scores, -1, keepdims=True)
    exp_scores = jnp.exp(scores - row_max)
    softmax_w = exp_scores / jnp.sum(exp_scores, -1, keepdims=True)
    weights_b = softmax_w.astype(jnp.bfloat16)
    recomputed = jnp.einsum(
        "kgqt,tkd->qkgd", weights_b, value_part, preferred_element_type=jnp.float32
    )
    row_delta = jnp.sum(cotangent.astype(jnp.float32) * recomputed, -1)
    grad_weights = jnp.einsum(
        "qkgd,tkd->kgqt", cotangent, value_part, preferred_element_type=jnp.float32
    )
    grad_scores = (
        softmax_w * (grad_weights - jnp.transpose(row_delta, (1, 2, 0))[..., None])
    ).astype(jnp.bfloat16)
    grad_q = (
        jnp.einsum("kgqt,tkd->qkgd", grad_scores, key_part, preferred_element_type=jnp.float32)
        * inv_root
    )
    grad_k = (
        jnp.einsum("kgqt,qkgd->tkd", grad_scores, queries, preferred_element_type=jnp.float32)
        * inv_root
    )
    grad_v = jnp.einsum("kgqt,qkgd->tkd", weights_b, cotangent, preferred_element_type=jnp.float32)
    grads = jnp.stack([grad_k, grad_v], 2)
    return (grad_q, grads.reshape(grads.shape[0], -1))


def split_halves(merged, head_index, level_bit):
    half_width = merged.shape[1] // 2
    lower_half = merged[:, :half_width]
    upper_half = merged[:, half_width:]
    upper_bit = head_index >> level_bit & 1
    kept_half = jnp.where(upper_bit == 1, upper_half, lower_half)
    sent_half = jnp.where(upper_bit == 1, lower_half, upper_half)
    return (kept_half, sent_half)


def general_device(query, key_value, grad_out, lengths, ancestors):
    col_width = key_value.shape[1]
    pair_width = 2 * HD
    rounds = (pair_width // col_width).bit_length() - 1 if col_width < pair_width else 0
    head_index = lax.axis_index("head")
    far_rows = (SEG_DEV - 1) * SLOT
    joined = key_value
    for level_bit in range(rounds):
        partner = from_partner(joined, "head", level_bit)
        upper_bit = head_index >> level_bit & 1
        joined = jnp.where(
            upper_bit == 1,
            jnp.concatenate([partner, joined], 1),
            jnp.concatenate([joined, partner], 1),
        )
    far_kv, far_lengths = (
        lax.all_gather(joined[:far_rows], "leaf", axis=0, tiled=True),
        lax.all_gather(lengths[: SEG_DEV - 1], "leaf", axis=0, tiled=True),
    )
    local_kv = joined.shape[1] // pair_width
    local_q = query.shape[1] // HD
    group_q = local_q // local_kv
    inv_root = HD ** (-0.5)
    positions = jnp.arange(SLOT)
    far_total = far_kv.shape[0]
    far_pieces = []
    far_starts = []
    own_parts = []
    grad_parts = []
    for slot_index in range(SEG_DEV):
        row_start = slot_index * SLOT
        row_valid = positions < lengths[slot_index]
        queries = query[row_start : row_start + SLOT].reshape(SLOT, local_kv, group_q, HD)
        cotangent = jnp.where(
            row_valid[:, None], grad_out[row_start : row_start + SLOT], jnp.zeros((), jnp.bfloat16)
        )
        cotangent = cotangent.reshape(SLOT, local_kv, group_q, HD)
        pieces = []
        key_masks = []
        slot_starts = []
        for level_index in range(slot_index):
            segment_id = ancestors[slot_index, level_index]
            block_index = segment_id // SEG_DEV * (SEG_DEV - 1) + segment_id % SEG_DEV
            block_start = block_index * SLOT
            pieces.append(lax.dynamic_slice_in_dim(far_kv, block_start, SLOT, 0))
            key_masks.append(
                jnp.broadcast_to(positions[None, :] < far_lengths[block_index], (SLOT, SLOT))
            )
            slot_starts.append(block_start)
        pieces.append(joined[row_start : row_start + SLOT])
        key_masks.append((positions[None, :] <= positions[:, None]) & row_valid[None, :])
        key_rows = jnp.concatenate(pieces, 0).reshape(-1, local_kv, 2, HD)
        grad_q, grad_kv = attend(
            queries, cotangent, key_rows, jnp.concatenate(key_masks, 1), inv_root
        )
        for level_index, block_start in enumerate(slot_starts):
            far_pieces.append(grad_kv[level_index * SLOT : (level_index + 1) * SLOT])
            far_starts.append(block_start)
        own_parts.append(grad_kv[slot_index * SLOT :])
        grad_parts.append(grad_q.reshape(SLOT, local_q * HD))
    far_grad = jnp.zeros((far_total, joined.shape[1]), jnp.float32)
    for piece, block_start in zip(far_pieces, far_starts):
        current = lax.dynamic_slice_in_dim(far_grad, block_start, SLOT, 0)
        far_grad = lax.dynamic_update_slice_in_dim(far_grad, current + piece, block_start, 0)
    merged = jnp.concatenate([far_grad] + own_parts, 0)
    for level_bit in reversed(range(rounds)):
        kept_half, sent_half = split_halves(merged, head_index, level_bit)
        merged = kept_half + from_partner(as_sent(sent_half), "head", level_bit).astype(
            sent_half.dtype
        )
    far_merged = merged[:far_total]
    own_sum = merged[far_total:]
    far_sum = lax.psum_scatter(
        far_merged.astype(jnp.bfloat16), "leaf", scatter_dimension=0, tiled=True
    ).astype(jnp.float32)
    combined = own_sum + jnp.concatenate([far_sum, jnp.zeros((SLOT, col_width), jnp.float32)], 0)
    return (jnp.concatenate(grad_parts, 0).astype(jnp.bfloat16), combined.astype(jnp.bfloat16))


FAR = SEG_DEV - 1
PAIRS = [(slot, level) for slot in range(SEG_DEV) for level in range(slot)]
F32 = jnp.float32
BF16 = jnp.bfloat16


def dot(left, right, left_dim, right_dim):
    return lax.dot_general(
        left, right, (((left_dim,), (right_dim,)), ((), ())), preferred_element_type=F32
    )


def kernel(n, kvh, group, lengths, ancestors, query, key_value, grad_out, dq_out, dkv_out, *scratch):
    scratch = list(scratch)
    kv_buf = [[scratch.pop(0) for _ in range(FAR)] for _ in range(kvh)]
    last_kv, q_buf, do_buf, dq_buf, dkv_buf, lens, own, term, sent, arrived = scratch[:10]
    kv_in, last_in, q_in, do_in, dq_sem, dkv_sem, kv_send, kv_recv, len_send, len_recv, g_send, g_recv = scratch[10:]
    me = lax.axis_index("leaf")
    inv_root = HD ** (-0.5)
    width = 2 * HD
    cols = group * HD

    def kv_local(h, l):
        return pltpu.make_async_copy(
            key_value.at[pl.ds(l * SLOT, SLOT), pl.ds(h * width, width)], kv_buf[h][l].at[me], kv_in.at[h, l]
        )

    def last_local(h):
        return pltpu.make_async_copy(
            key_value.at[pl.ds(FAR * SLOT, SLOT), pl.ds(h * width, width)], last_kv.at[h], last_in.at[h]
        )

    def rows_in(source, target, sem, j):
        rows = pl.ds(j * SLOT, SLOT)
        return pltpu.make_async_copy(source.at[rows], target.at[rows], sem.at[j])

    for h in range(kvh):
        for l in range(FAR):
            kv_local(h, l).start()
    for h in range(kvh):
        last_local(h).start()
    for j in range(SEG_DEV):
        rows_in(query, q_buf, q_in, j).start()
        rows_in(grad_out, do_buf, do_in, j).start()

    barrier = pltpu.get_barrier_semaphore()
    for k in range(1, n):
        pl.semaphore_signal(
            barrier, inc=1, device_id={"leaf": lax.rem(me + k, n)}, device_id_type=pl.DeviceIdType.MESH
        )
    for l in range(FAR):
        lens[me, l] = jnp.full((128,), lengths[l], jnp.int32)
    pl.semaphore_wait(barrier, n - 1)

    def lens_copy(k):
        return pltpu.make_async_remote_copy(
            src_ref=lens.at[me],
            dst_ref=lens.at[me],
            send_sem=len_send.at[k - 1],
            recv_sem=len_recv.at[k - 1],
            device_id={"leaf": lax.rem(me + k, n)},
            device_id_type=pl.DeviceIdType.MESH,
        )

    def hop_ok(way, s):
        if way == 0:
            return (me < n - 1) & (me - s >= 0)
        return (me > 0) & (me + s <= n - 1)

    def got_ok(way, s):
        return me - 1 - s >= 0 if way == 0 else me + 1 + s <= n - 1

    def kv_copy(way, s, h, l, block):
        ref = kv_buf[h][l].at[block]
        return pltpu.make_async_remote_copy(
            src_ref=ref,
            dst_ref=ref,
            send_sem=kv_send.at[way, s, h, l],
            recv_sem=kv_recv.at[way, s, h, l],
            device_id={"leaf": me + 1 if way == 0 else me - 1},
            device_id_type=pl.DeviceIdType.MESH,
        )

    def kv_start(way, s, h, l):
        @pl.when(hop_ok(way, s))
        def _():
            kv_copy(way, s, h, l, me - s if way == 0 else me + s).start()

    def kv_arrive(way, s, h, l):
        @pl.when(got_ok(way, s))
        def _():
            kv_copy(way, s, h, l, me - 1 - s if way == 0 else me + 1 + s).wait_recv()

    def own_sends(h):
        for l in range(FAR):
            kv_start(0, 0, h, l)
            kv_start(1, 0, h, l)

    def hop(h, s):
        for l in range(FAR):
            for way in (0, 1):
                kv_arrive(way, s, h, l)
                if s + 1 < n - 1:
                    kv_start(way, s + 1, h, l)

    key_pos = lax.broadcasted_iota(jnp.int32, (SLOT, 128), 0)
    query_pos = lax.broadcasted_iota(jnp.int32, (SLOT, 128), 1) & (SLOT - 1)
    parts = 2 if group % 4 == 0 else 1
    heads = group // parts
    lanes = heads * SLOT

    def wide(tile):
        return jnp.concatenate([tile] * (lanes // 128), 1)

    def home(j, l):
        return lax.div(ancestors[j, l], SEG_DEV)

    def dq_copy(h, j):
        view = (pl.ds(j * SLOT, SLOT), pl.ds(h * cols, cols))
        return pltpu.make_async_copy(dq_buf.at[view], dq_out.at[view], dq_sem.at[h, j])

    def compute(h, j):
        rows = pl.ds(j * SLOT, SLOT)
        pieces, biases = [], []
        for l in range(j):
            place = home(j, l)
            pieces.append(kv_buf[h][l][place])
            biases.append(jnp.where(key_pos < lens[place, l : l + 1, :], 0.0, masked_score))
        pieces.append(kv_buf[h][j][me] if j < FAR else last_kv[h])
        biases.append(
            jnp.where((key_pos < lengths[j]) & (key_pos <= query_pos), 0.0, masked_score)
        )
        keys = jnp.concatenate([piece[:, :HD] for piece in pieces], 0)
        values = jnp.concatenate([piece[:, HD:] for piece in pieces], 0)
        bias = wide(jnp.concatenate(biases, 0))
        valid = jnp.where(key_pos < lengths[j], 1.0, 0.0).astype(BF16)
        grad_k = grad_v = None
        for part in range(parts):
            at = [(h * group + part * heads + g) * HD for g in range(heads)]
            q = jnp.concatenate([q_buf[rows, pl.ds(a, HD)] for a in at], 0)
            do = jnp.concatenate([do_buf[rows, pl.ds(a, HD)] * valid for a in at], 0)
            scores = dot(keys, q, 1, 1) * (inv_root * math.log2(math.e)) + bias
            top = jnp.max(scores, 0, keepdims=True)
            powers = jnp.exp2(scores - top)
            probs = powers * (1.0 / jnp.sum(powers, 0, keepdims=True))
            probs_b = probs.astype(BF16)
            dprobs = dot(values, do, 1, 1)
            delta = jnp.sum(probs_b.astype(F32) * dprobs, 0, keepdims=True)
            dscores = (probs * (dprobs - delta)).astype(BF16)
            part_v = dot(probs_b, do, 1, 0)
            part_k = dot(dscores, q, 1, 0)
            grad_v = part_v if grad_v is None else grad_v + part_v
            grad_k = part_k if grad_k is None else grad_k + part_k
            grad_q = (dot(dscores, keys, 0, 0) * inv_root).astype(BF16)
            for g, a in enumerate(at):
                dq_buf[rows, pl.ds(a, HD)] = grad_q[g * SLOT : (g + 1) * SLOT]
        dq_copy(h, j).start()
        grads = jnp.concatenate([grad_k * inv_root, grad_v], 1)
        for l in range(j):
            term[h, PAIRS.index((j, l))] = grads[l * SLOT : (l + 1) * SLOT]
        own[h, j] = grads[j * SLOT :]

    def local_terms(h, l, target):
        total = None
        for j in range(l + 1, SEG_DEV):
            weight = jnp.where(home(j, l) == target, 1.0, 0.0).astype(F32)
            one = term[h, PAIRS.index((j, l))] * weight
            total = one if total is None else total + one
        return total

    def g_copy(way, k, h, l, target):
        return pltpu.make_async_remote_copy(
            src_ref=sent.at[h, target, l],
            dst_ref=arrived.at[way, h, target, l],
            send_sem=g_send.at[way, k - 1, h, l],
            recv_sem=g_recv.at[way, k - 1, h, l],
            device_id={"leaf": me + 1 if way == 0 else me - 1},
            device_id_type=pl.DeviceIdType.MESH,
        )

    def g_target(way, k):
        return me + k if way == 0 else me - k

    def g_ok(way, k):
        return me + k <= n - 1 if way == 0 else me - k >= 0

    def g_behind(way):
        return me > 0 if way == 0 else me < n - 1

    def send_terms(h, k):
        for l in range(FAR):
            for way in (0, 1):
                @pl.when(g_ok(way, k))
                def _():
                    target = g_target(way, k)
                    sent[h, target, l] = local_terms(h, l, target).astype(BF16)

                    if k < n - 1:
                        @pl.when(g_behind(way))
                        def _():
                            g_copy(way, k + 1, h, l, target).wait_recv()
                            total = sent[h, target, l].astype(F32) + arrived[way, h, target, l].astype(F32)
                            sent[h, target, l] = total.astype(BF16)

                    g_copy(way, k, h, l, target).start()

    def dkv_copy(h, j):
        view = (pl.ds(j * SLOT, SLOT), pl.ds(h * width, width))
        return pltpu.make_async_copy(dkv_buf.at[view], dkv_out.at[view], dkv_sem.at[h, j])

    def finish_last(h):
        dkv_buf[pl.ds(FAR * SLOT, SLOT), pl.ds(h * width, width)] = own[h, FAR].astype(BF16)
        dkv_copy(h, FAR).start()

    def finish(h):
        for l in range(FAR):
            own[h, l] = own[h, l] + local_terms(h, l, me).astype(BF16).astype(F32)
            for way in (0, 1):
                @pl.when(g_behind(way))
                def _():
                    g_copy(way, 1, h, l, me).wait_recv()
                    own[h, l] = own[h, l] + arrived[way, h, me, l].astype(F32)
            dkv_buf[pl.ds(l * SLOT, SLOT), pl.ds(h * width, width)] = own[h, l].astype(BF16)
            dkv_copy(h, l).start()

    for k in range(1, n):
        lens_copy(k).start()
    for l in range(FAR):
        kv_local(0, l).wait()
        kv_start(0, 0, 0, l)
        kv_start(1, 0, 0, l)
    for h in range(1, kvh):
        for l in range(FAR):
            kv_local(h, l).wait()
    for h in range(kvh):
        last_local(h).wait()
    for k in range(1, n):
        lens_copy(k).wait()
    for j in range(SEG_DEV):
        rows_in(query, q_buf, q_in, j).wait()
        rows_in(grad_out, do_buf, do_in, j).wait()

    for h in range(kvh):
        compute(h, 0)
    for s in range(n - 1):
        hop(0, s)
    for h in range(kvh):
        steps = []
        if h + 1 < kvh:
            own_sends(h + 1)
            steps += [functools.partial(hop, h + 1, s) for s in range(n - 1)]
        if h > 0:
            steps += [functools.partial(send_terms, h - 1, k) for k in range(n - 1, 0, -1)]
        for j in range(1, SEG_DEV):
            if steps and h > 0:
                steps.pop(0)()
            compute(h, j)
            if steps and h == 0:
                steps.pop(0)()
        for step in steps:
            step()
        finish_last(h)
    for k in range(n - 1, 0, -1):
        send_terms(kvh - 1, k)
    for h in range(kvh):
        finish(h)

    for k in range(1, n):
        for way in (0, 1):
            @pl.when(g_ok(way, k))
            def _():
                for h in range(kvh):
                    for l in range(FAR):
                        g_copy(way, k, h, l, g_target(way, k)).wait_send()
    for s in range(n - 1):
        for way in (0, 1):
            @pl.when(hop_ok(way, s))
            def _():
                for h in range(kvh):
                    for l in range(FAR):
                        kv_copy(way, s, h, l, me - s if way == 0 else me + s).wait_send()
    for h in range(kvh):
        for j in range(SEG_DEV):
            dq_copy(h, j).wait()
            dkv_copy(h, j).wait()


def line_device(query, key_value, grad_out, lengths, ancestors):
    n = lax.axis_size("leaf")
    width = 2 * HD
    kvh = key_value.shape[1] // width
    group = query.shape[1] // (kvh * HD)
    tile = (SLOT, width)
    scratch = [pltpu.VMEM((n,) + tile, BF16) for _ in range(kvh * FAR)]
    scratch += [
        pltpu.VMEM((kvh,) + tile, BF16),
        pltpu.VMEM(query.shape, BF16),
        pltpu.VMEM(query.shape, BF16),
        pltpu.VMEM(query.shape, BF16),
        pltpu.VMEM(key_value.shape, BF16),
        pltpu.VMEM((n, 8, 128), jnp.int32),
        pltpu.VMEM((kvh, SEG_DEV) + tile, F32),
        pltpu.VMEM((kvh, len(PAIRS)) + tile, F32),
        pltpu.VMEM((kvh, n, FAR) + tile, BF16),
        pltpu.VMEM((2, kvh, n, FAR) + tile, BF16),
    ]
    dma = pltpu.SemaphoreType.DMA
    scratch += [dma((kvh, FAR)), dma((kvh,)), dma((SEG_DEV,)), dma((SEG_DEV,))]
    scratch += [dma((kvh, SEG_DEV)), dma((kvh, SEG_DEV))]
    scratch += [dma((2, n - 1, kvh, FAR)), dma((2, n - 1, kvh, FAR)), dma((n - 1,)), dma((n - 1,))]
    scratch += [dma((2, n - 1, kvh, FAR)), dma((2, n - 1, kvh, FAR))]
    smem = pl.BlockSpec(memory_space=pltpu.SMEM)
    anywhere = pl.BlockSpec(memory_space=pl.ANY)
    return pl.pallas_call(
        functools.partial(kernel, n, kvh, group),
        out_shape=(
            jax.ShapeDtypeStruct(query.shape, BF16),
            jax.ShapeDtypeStruct(key_value.shape, BF16),
        ),
        in_specs=[smem, smem, anywhere, anywhere, anywhere],
        out_specs=(anywhere, anywhere),
        scratch_shapes=scratch,
        compiler_params=pltpu.CompilerParams(
            collective_id=0, has_side_effects=True, vmem_limit_bytes=48 * 1024 * 1024
        ),
    )(lengths, ancestors, query, key_value, grad_out)


def on_device(query, key_value, grad_out, lengths, ancestors):
    whole_heads = key_value.shape[1] % (2 * HD) == 0
    step = line_device if whole_heads else general_device
    return step(query, key_value, grad_out, lengths, ancestors)


def solution(mesh):
    return jax.shard_map(
        on_device,
        mesh=mesh,
        in_specs=(
            P(("grp", "leaf"), "head"),
            P(("grp", "leaf"), "head"),
            P(("grp", "leaf"), "head"),
            P(("grp", "leaf")),
            P(("grp", "leaf"), None),
        ),
        out_specs=(P(("grp", "leaf"), "head"), P(("grp", "leaf"), "head")),
        check_vma=False,
    )
```

```python
import functools
import math

import jax
import jax.numpy as jnp
from jax import lax
from jax.experimental import pallas as pl
from jax.experimental.pallas import tpu as pltpu
from jax.sharding import PartitionSpec as P

HD = 128
SLOT = 64
SEG_DEV = 5


masked_score = -1e30


def from_partner(block, axis, bit):
    count = lax.axis_size(axis)
    route = []
    for low in range(count):
        high = low | 1 << bit
        if high != low and high < count:
            route += [(low, high), (high, low)]
    return lax.ppermute(block, axis, route)


def as_sent(array):

    def short(part):
        return part.astype(jnp.bfloat16) if part.dtype == jnp.float32 else part

    return jax.tree.map(short, array)


def attend(queries, cotangent, key_rows, allowed, inv_root):
    key_part = key_rows[:, :, 0]
    value_part = key_rows[:, :, 1]
    scores = (
        jnp.einsum("qkgd,tkd->kgqt", queries, key_part, preferred_element_type=jnp.float32)
        * inv_root
    )
    scores = jnp.where(allowed, scores, masked_score)
    row_max = jnp.max(scores, -1, keepdims=True)
    exp_scores = jnp.exp(scores - row_max)
    softmax_w = exp_scores / jnp.sum(exp_scores, -1, keepdims=True)
    weights_b = softmax_w.astype(jnp.bfloat16)
    recomputed = jnp.einsum(
        "kgqt,tkd->qkgd", weights_b, value_part, preferred_element_type=jnp.float32
    )
    row_delta = jnp.sum(cotangent.astype(jnp.float32) * recomputed, -1)
    grad_weights = jnp.einsum(
        "qkgd,tkd->kgqt", cotangent, value_part, preferred_element_type=jnp.float32
    )
    grad_scores = (
        softmax_w * (grad_weights - jnp.transpose(row_delta, (1, 2, 0))[..., None])
    ).astype(jnp.bfloat16)
    grad_q = (
        jnp.einsum("kgqt,tkd->qkgd", grad_scores, key_part, preferred_element_type=jnp.float32)
        * inv_root
    )
    grad_k = (
        jnp.einsum("kgqt,qkgd->tkd", grad_scores, queries, preferred_element_type=jnp.float32)
        * inv_root
    )
    grad_v = jnp.einsum("kgqt,qkgd->tkd", weights_b, cotangent, preferred_element_type=jnp.float32)
    grads = jnp.stack([grad_k, grad_v], 2)
    return (grad_q, grads.reshape(grads.shape[0], -1))


def split_halves(merged, head_index, level_bit):
    half_width = merged.shape[1] // 2
    lower_half = merged[:, :half_width]
    upper_half = merged[:, half_width:]
    upper_bit = head_index >> level_bit & 1
    kept_half = jnp.where(upper_bit == 1, upper_half, lower_half)
    sent_half = jnp.where(upper_bit == 1, lower_half, upper_half)
    return (kept_half, sent_half)


def general_device(query, key_value, grad_out, lengths, ancestors):
    col_width = key_value.shape[1]
    pair_width = 2 * HD
    rounds = (pair_width // col_width).bit_length() - 1 if col_width < pair_width else 0
    head_index = lax.axis_index("head")
    far_rows = (SEG_DEV - 1) * SLOT
    joined = key_value
    for level_bit in range(rounds):
        partner = from_partner(joined, "head", level_bit)
        upper_bit = head_index >> level_bit & 1
        joined = jnp.where(
            upper_bit == 1,
            jnp.concatenate([partner, joined], 1),
            jnp.concatenate([joined, partner], 1),
        )
    far_kv, far_lengths = (
        lax.all_gather(joined[:far_rows], "leaf", axis=0, tiled=True),
        lax.all_gather(lengths[: SEG_DEV - 1], "leaf", axis=0, tiled=True),
    )
    local_kv = joined.shape[1] // pair_width
    local_q = query.shape[1] // HD
    group_q = local_q // local_kv
    inv_root = HD ** (-0.5)
    positions = jnp.arange(SLOT)
    far_total = far_kv.shape[0]
    far_pieces = []
    far_starts = []
    own_parts = []
    grad_parts = []
    for slot_index in range(SEG_DEV):
        row_start = slot_index * SLOT
        row_valid = positions < lengths[slot_index]
        queries = query[row_start : row_start + SLOT].reshape(SLOT, local_kv, group_q, HD)
        cotangent = jnp.where(
            row_valid[:, None], grad_out[row_start : row_start + SLOT], jnp.zeros((), jnp.bfloat16)
        )
        cotangent = cotangent.reshape(SLOT, local_kv, group_q, HD)
        pieces = []
        key_masks = []
        slot_starts = []
        for level_index in range(slot_index):
            segment_id = ancestors[slot_index, level_index]
            block_index = segment_id // SEG_DEV * (SEG_DEV - 1) + segment_id % SEG_DEV
            block_start = block_index * SLOT
            pieces.append(lax.dynamic_slice_in_dim(far_kv, block_start, SLOT, 0))
            key_masks.append(
                jnp.broadcast_to(positions[None, :] < far_lengths[block_index], (SLOT, SLOT))
            )
            slot_starts.append(block_start)
        pieces.append(joined[row_start : row_start + SLOT])
        key_masks.append((positions[None, :] <= positions[:, None]) & row_valid[None, :])
        key_rows = jnp.concatenate(pieces, 0).reshape(-1, local_kv, 2, HD)
        grad_q, grad_kv = attend(
            queries, cotangent, key_rows, jnp.concatenate(key_masks, 1), inv_root
        )
        for level_index, block_start in enumerate(slot_starts):
            far_pieces.append(grad_kv[level_index * SLOT : (level_index + 1) * SLOT])
            far_starts.append(block_start)
        own_parts.append(grad_kv[slot_index * SLOT :])
        grad_parts.append(grad_q.reshape(SLOT, local_q * HD))
    far_grad = jnp.zeros((far_total, joined.shape[1]), jnp.float32)
    for piece, block_start in zip(far_pieces, far_starts):
        current = lax.dynamic_slice_in_dim(far_grad, block_start, SLOT, 0)
        far_grad = lax.dynamic_update_slice_in_dim(far_grad, current + piece, block_start, 0)
    merged = jnp.concatenate([far_grad] + own_parts, 0)
    for level_bit in reversed(range(rounds)):
        kept_half, sent_half = split_halves(merged, head_index, level_bit)
        merged = kept_half + from_partner(as_sent(sent_half), "head", level_bit).astype(
            sent_half.dtype
        )
    far_merged = merged[:far_total]
    own_sum = merged[far_total:]
    far_sum = lax.psum_scatter(
        far_merged.astype(jnp.bfloat16), "leaf", scatter_dimension=0, tiled=True
    ).astype(jnp.float32)
    combined = own_sum + jnp.concatenate([far_sum, jnp.zeros((SLOT, col_width), jnp.float32)], 0)
    return (jnp.concatenate(grad_parts, 0).astype(jnp.bfloat16), combined.astype(jnp.bfloat16))


FAR = SEG_DEV - 1
PAIRS = [(slot, level) for slot in range(SEG_DEV) for level in range(slot)]
F32 = jnp.float32
BF16 = jnp.bfloat16


def dot(left, right, left_dim, right_dim):
    return lax.dot_general(
        left, right, (((left_dim,), (right_dim,)), ((), ())), preferred_element_type=F32
    )


def kernel(n, kvh, group, lengths_in, ancestors_in, query, key_value, grad_out, dq_out, dkv_out, *scratch):
    scratch = list(scratch)
    lengths, ancestors, tree_in = scratch.pop(0), scratch.pop(0), scratch.pop(0)
    kv_buf = [[scratch.pop(0) for _ in range(FAR)] for _ in range(kvh)]
    last_kv, q_buf, do_buf, dq_buf, dkv_buf, lens, own, term, sent, arrived = scratch[:10]
    kv_in, last_in, q_in, do_in, dq_sem, dkv_sem, kv_send, kv_recv, len_send, len_recv, g_send, g_recv = scratch[10:]
    me = lax.axis_index("leaf")
    inv_root = HD ** (-0.5)
    width = 2 * HD
    cols = group * HD

    def kv_local(h, l):
        return pltpu.make_async_copy(
            key_value.at[pl.ds(l * SLOT, SLOT), pl.ds(h * width, width)], kv_buf[h][l].at[me], kv_in.at[h, l]
        )

    def last_local(h):
        return pltpu.make_async_copy(
            key_value.at[pl.ds(FAR * SLOT, SLOT), pl.ds(h * width, width)], last_kv.at[h], last_in.at[h]
        )

    def rows_in(source, target, sem, j):
        rows = pl.ds(j * SLOT, SLOT)
        return pltpu.make_async_copy(source.at[rows], target.at[rows], sem.at[j])

    tree = [
        pltpu.make_async_copy(lengths_in, lengths, tree_in.at[0]),
        pltpu.make_async_copy(ancestors_in, ancestors, tree_in.at[1]),
    ]
    for copy in tree:
        copy.start()
    for h in range(kvh):
        for l in range(FAR):
            kv_local(h, l).start()
    for h in range(kvh):
        last_local(h).start()
    for j in range(SEG_DEV):
        rows_in(query, q_buf, q_in, j).start()
        rows_in(grad_out, do_buf, do_in, j).start()

    barrier = pltpu.get_barrier_semaphore()
    for k in range(1, n):
        pl.semaphore_signal(
            barrier, inc=1, device_id={"leaf": lax.rem(me + k, n)}, device_id_type=pl.DeviceIdType.MESH
        )
    for copy in tree:
        copy.wait()
    for l in range(FAR):
        lens[me, l] = jnp.full((128,), lengths[l], jnp.int32)
    pl.semaphore_wait(barrier, n - 1)

    def lens_copy(k):
        return pltpu.make_async_remote_copy(
            src_ref=lens.at[me],
            dst_ref=lens.at[me],
            send_sem=len_send.at[k - 1],
            recv_sem=len_recv.at[k - 1],
            device_id={"leaf": lax.rem(me + k, n)},
            device_id_type=pl.DeviceIdType.MESH,
        )

    def hop_ok(way, s):
        if way == 0:
            return (me < n - 1) & (me - s >= 0)
        return (me > 0) & (me + s <= n - 1)

    def got_ok(way, s):
        return me - 1 - s >= 0 if way == 0 else me + 1 + s <= n - 1

    def kv_copy(way, s, h, l, block):
        ref = kv_buf[h][l].at[block]
        return pltpu.make_async_remote_copy(
            src_ref=ref,
            dst_ref=ref,
            send_sem=kv_send.at[way, s, h, l],
            recv_sem=kv_recv.at[way, s, h, l],
            device_id={"leaf": me + 1 if way == 0 else me - 1},
            device_id_type=pl.DeviceIdType.MESH,
        )

    def kv_start(way, s, h, l):
        @pl.when(hop_ok(way, s))
        def _():
            kv_copy(way, s, h, l, me - s if way == 0 else me + s).start()

    def kv_arrive(way, s, h, l):
        @pl.when(got_ok(way, s))
        def _():
            kv_copy(way, s, h, l, me - 1 - s if way == 0 else me + 1 + s).wait_recv()

    def own_sends(h, sends):
        if h == kvh:
            return
        for way in (0, 1):
            before = me if way == 0 else n - 1 - me

            @pl.when((before == sends) & hop_ok(way, 0))
            def _():
                for l in range(FAR):
                    kv_copy(way, 0, h, l, me).start()

    def hop(h, s):
        for l in range(FAR):
            for way in (0, 1):
                kv_arrive(way, s, h, l)
                if s + 1 < n - 1:
                    kv_start(way, s + 1, h, l)
        own_sends(h + 1, s + 1)

    key_pos = lax.broadcasted_iota(jnp.int32, (SLOT, 128), 0)
    query_pos = lax.broadcasted_iota(jnp.int32, (SLOT, 128), 1) & (SLOT - 1)
    parts = 2 if group % 4 == 0 else 1
    heads = group // parts
    lanes = heads * SLOT

    def wide(tile):
        return jnp.concatenate([tile] * (lanes // 128), 1)

    def home(j, l):
        return lax.div(ancestors[l, j], SEG_DEV)

    def dq_copy(h, j):
        view = (pl.ds(j * SLOT, SLOT), pl.ds(h * cols, cols))
        return pltpu.make_async_copy(dq_buf.at[view], dq_out.at[view], dq_sem.at[h, j])

    def compute(h, j):
        rows = pl.ds(j * SLOT, SLOT)
        pieces, biases = [], []
        for l in range(j):
            place = home(j, l)
            pieces.append(kv_buf[h][l][place])
            biases.append(jnp.where(key_pos < lens[place, l : l + 1, :], 0.0, masked_score))
        pieces.append(kv_buf[h][j][me] if j < FAR else last_kv[h])
        biases.append(
            jnp.where((key_pos < lengths[j]) & (key_pos <= query_pos), 0.0, masked_score)
        )
        keys = jnp.concatenate([piece[:, :HD] for piece in pieces], 0)
        values = jnp.concatenate([piece[:, HD:] for piece in pieces], 0)
        bias = wide(jnp.concatenate(biases, 0))
        valid = jnp.where(key_pos < lengths[j], 1.0, 0.0).astype(BF16)
        grad_k = grad_v = None
        for part in range(parts):
            at = [(h * group + part * heads + g) * HD for g in range(heads)]
            q = jnp.concatenate([q_buf[rows, pl.ds(a, HD)] for a in at], 0)
            do = jnp.concatenate([do_buf[rows, pl.ds(a, HD)] * valid for a in at], 0)
            scores = dot(keys, q, 1, 1) * (inv_root * math.log2(math.e)) + bias
            top = jnp.max(scores, 0, keepdims=True)
            powers = jnp.exp2(scores - top)
            probs = powers * (1.0 / jnp.sum(powers, 0, keepdims=True))
            probs_b = probs.astype(BF16)
            dprobs = dot(values, do, 1, 1)
            delta = jnp.sum(probs_b.astype(F32) * dprobs, 0, keepdims=True)
            dscores = (probs * (dprobs - delta)).astype(BF16)
            part_v = dot(probs_b, do, 1, 0)
            part_k = dot(dscores, q, 1, 0)
            grad_v = part_v if grad_v is None else grad_v + part_v
            grad_k = part_k if grad_k is None else grad_k + part_k
            grad_q = (dot(dscores, keys, 0, 0) * inv_root).astype(BF16)
            for g, a in enumerate(at):
                dq_buf[rows, pl.ds(a, HD)] = grad_q[g * SLOT : (g + 1) * SLOT]
        dq_copy(h, j).start()
        grads = jnp.concatenate([grad_k * inv_root, grad_v], 1)
        for l in range(j):
            term[h, PAIRS.index((j, l))] = grads[l * SLOT : (l + 1) * SLOT]
        own[h, j] = grads[j * SLOT :]

    def local_terms(h, l, target):
        total = None
        for j in range(l + 1, SEG_DEV):
            weight = jnp.where(home(j, l) == target, 1.0, 0.0).astype(F32)
            one = term[h, PAIRS.index((j, l))] * weight
            total = one if total is None else total + one
        return total

    def g_copy(way, k, h, l, target):
        return pltpu.make_async_remote_copy(
            src_ref=sent.at[h, target, l],
            dst_ref=arrived.at[way, h, target, l],
            send_sem=g_send.at[way, k - 1, h, l],
            recv_sem=g_recv.at[way, k - 1, h, l],
            device_id={"leaf": me + 1 if way == 0 else me - 1},
            device_id_type=pl.DeviceIdType.MESH,
        )

    def g_target(way, k):
        return me + k if way == 0 else me - k

    def g_ok(way, k):
        return me + k <= n - 1 if way == 0 else me - k >= 0

    def g_behind(way):
        return me > 0 if way == 0 else me < n - 1

    def send_terms(h, k, l):
        for way in (0, 1):
            @pl.when(g_ok(way, k))
            def _():
                target = g_target(way, k)
                sent[h, target, l] = local_terms(h, l, target).astype(BF16)

                if k < n - 1:
                    @pl.when(g_behind(way))
                    def _():
                        g_copy(way, k + 1, h, l, target).wait_recv()
                        total = sent[h, target, l].astype(F32) + arrived[way, h, target, l].astype(F32)
                        sent[h, target, l] = total.astype(BF16)

                g_copy(way, k, h, l, target).start()

    def dkv_copy(h, j):
        view = (pl.ds(j * SLOT, SLOT), pl.ds(h * width, width))
        return pltpu.make_async_copy(dkv_buf.at[view], dkv_out.at[view], dkv_sem.at[h, j])

    def finish_last(h):
        dkv_buf[pl.ds(FAR * SLOT, SLOT), pl.ds(h * width, width)] = own[h, FAR].astype(BF16)
        dkv_copy(h, FAR).start()

    def finish(h, l):
        own[h, l] = own[h, l] + local_terms(h, l, me).astype(BF16).astype(F32)
        for way in (0, 1):
            @pl.when(g_behind(way))
            def _():
                g_copy(way, 1, h, l, me).wait_recv()
                own[h, l] = own[h, l] + arrived[way, h, me, l].astype(F32)
        dkv_buf[pl.ds(l * SLOT, SLOT), pl.ds(h * width, width)] = own[h, l].astype(BF16)
        dkv_copy(h, l).start()

    for k in range(1, n):
        lens_copy(k).start()
    for l in range(FAR):
        kv_local(0, l).wait()
        kv_start(0, 0, 0, l)
        kv_start(1, 0, 0, l)
    for h in range(1, kvh):
        for l in range(FAR):
            kv_local(h, l).wait()
    own_sends(1, 0)
    for h in range(kvh):
        last_local(h).wait()
    for k in range(1, n):
        lens_copy(k).wait()
    for j in range(SEG_DEV):
        rows_in(query, q_buf, q_in, j).wait()
        rows_in(grad_out, do_buf, do_in, j).wait()

    for h in range(kvh):
        compute(h, 0)
    for s in range(n - 1):
        hop(0, s)

    order = [(h, j) for h in range(kvh) for j in range(FAR, 0, -1)]
    for step in range(len(order) + n):
        if step < len(order):
            h, j = order[step]
            compute(h, j)
            if h + 1 < kvh and FAR - j < n - 2:
                hop(h + 1, FAR - j)
        for k in range(n - 1, 0, -1):
            behind = step - (n - 1 - k)
            if 0 <= behind < len(order):
                done_h, done_j = order[behind]
                send_terms(done_h, k, done_j - 1)
        behind = step - n
        if 0 <= behind < len(order):
            done_h, done_j = order[behind]
            finish(done_h, done_j - 1)
        if step < len(order):
            h, j = order[step]
            if j == 1:
                finish_last(h)
                for s in range(n - 2 if FAR > n - 2 else FAR, n - 1):
                    if h + 1 < kvh:
                        hop(h + 1, s)

    for k in range(1, n):
        for way in (0, 1):
            @pl.when(g_ok(way, k))
            def _():
                for h in range(kvh):
                    for l in range(FAR):
                        g_copy(way, k, h, l, g_target(way, k)).wait_send()
    for s in range(n - 1):
        for way in (0, 1):
            @pl.when(hop_ok(way, s))
            def _():
                for h in range(kvh):
                    for l in range(FAR):
                        kv_copy(way, s, h, l, me - s if way == 0 else me + s).wait_send()
    for h in range(kvh):
        for j in range(SEG_DEV):
            dq_copy(h, j).wait()
            dkv_copy(h, j).wait()


def line_device(query, key_value, grad_out, lengths, ancestors):
    n = lax.axis_size("leaf")
    width = 2 * HD
    kvh = key_value.shape[1] // width
    group = query.shape[1] // (kvh * HD)
    tile = (SLOT, width)
    dma = pltpu.SemaphoreType.DMA
    scratch = [
        pltpu.SMEM(lengths.shape, jnp.int32),
        pltpu.SMEM(ancestors.shape[::-1], jnp.int32),
        dma((2,)),
    ]
    scratch += [pltpu.VMEM((n,) + tile, BF16) for _ in range(kvh * FAR)]
    scratch += [
        pltpu.VMEM((kvh,) + tile, BF16),
        pltpu.VMEM(query.shape, BF16),
        pltpu.VMEM(query.shape, BF16),
        pltpu.VMEM(query.shape, BF16),
        pltpu.VMEM(key_value.shape, BF16),
        pltpu.VMEM((n, 8, 128), jnp.int32),
        pltpu.VMEM((kvh, SEG_DEV) + tile, F32),
        pltpu.VMEM((kvh, len(PAIRS)) + tile, F32),
        pltpu.VMEM((kvh, n, FAR) + tile, BF16),
        pltpu.VMEM((2, kvh, n, FAR) + tile, BF16),
    ]
    scratch += [dma((kvh, FAR)), dma((kvh,)), dma((SEG_DEV,)), dma((SEG_DEV,))]
    scratch += [dma((kvh, SEG_DEV)), dma((kvh, SEG_DEV))]
    scratch += [dma((2, n - 1, kvh, FAR)), dma((2, n - 1, kvh, FAR)), dma((n - 1,)), dma((n - 1,))]
    scratch += [dma((2, n - 1, kvh, FAR)), dma((2, n - 1, kvh, FAR))]
    anywhere = pl.BlockSpec(memory_space=pl.ANY)
    return pl.pallas_call(
        functools.partial(kernel, n, kvh, group),
        out_shape=(
            jax.ShapeDtypeStruct(query.shape, BF16),
            jax.ShapeDtypeStruct(key_value.shape, BF16),
        ),
        in_specs=[anywhere] * 5,
        out_specs=(anywhere, anywhere),
        scratch_shapes=scratch,
        compiler_params=pltpu.CompilerParams(
            collective_id=0, has_side_effects=True, vmem_limit_bytes=60 * 1024 * 1024
        ),
    )(lengths, ancestors.T, query, key_value, grad_out)


def on_device(query, key_value, grad_out, lengths, ancestors):
    whole_heads = key_value.shape[1] % (2 * HD) == 0
    step = line_device if whole_heads else general_device
    return step(query, key_value, grad_out, lengths, ancestors)


def solution(mesh):
    return jax.shard_map(
        on_device,
        mesh=mesh,
        in_specs=(
            P(("grp", "leaf"), "head"),
            P(("grp", "leaf"), "head"),
            P(("grp", "leaf"), "head"),
            P(("grp", "leaf")),
            P(("grp", "leaf"), None),
        ),
        out_specs=(P(("grp", "leaf"), "head"), P(("grp", "leaf"), "head")),
        check_vma=False,
    )
```

```python
import functools
import math

import jax
import jax.numpy as jnp
from jax import lax
from jax.experimental import pallas as pl
from jax.experimental.pallas import tpu as pltpu
from jax.sharding import PartitionSpec as P

HD = 128
SLOT = 64
SEG_DEV = 5


masked_score = -1e30


def from_partner(block, axis, bit):
    count = lax.axis_size(axis)
    route = []
    for low in range(count):
        high = low | 1 << bit
        if high != low and high < count:
            route += [(low, high), (high, low)]
    return lax.ppermute(block, axis, route)


def as_sent(array):

    def short(part):
        return part.astype(jnp.bfloat16) if part.dtype == jnp.float32 else part

    return jax.tree.map(short, array)


def attend(queries, cotangent, key_rows, allowed, inv_root):
    key_part = key_rows[:, :, 0]
    value_part = key_rows[:, :, 1]
    scores = (
        jnp.einsum("qkgd,tkd->kgqt", queries, key_part, preferred_element_type=jnp.float32)
        * inv_root
    )
    scores = jnp.where(allowed, scores, masked_score)
    row_max = jnp.max(scores, -1, keepdims=True)
    exp_scores = jnp.exp(scores - row_max)
    softmax_w = exp_scores / jnp.sum(exp_scores, -1, keepdims=True)
    weights_b = softmax_w.astype(jnp.bfloat16)
    recomputed = jnp.einsum(
        "kgqt,tkd->qkgd", weights_b, value_part, preferred_element_type=jnp.float32
    )
    row_delta = jnp.sum(cotangent.astype(jnp.float32) * recomputed, -1)
    grad_weights = jnp.einsum(
        "qkgd,tkd->kgqt", cotangent, value_part, preferred_element_type=jnp.float32
    )
    grad_scores = (
        softmax_w * (grad_weights - jnp.transpose(row_delta, (1, 2, 0))[..., None])
    ).astype(jnp.bfloat16)
    grad_q = (
        jnp.einsum("kgqt,tkd->qkgd", grad_scores, key_part, preferred_element_type=jnp.float32)
        * inv_root
    )
    grad_k = (
        jnp.einsum("kgqt,qkgd->tkd", grad_scores, queries, preferred_element_type=jnp.float32)
        * inv_root
    )
    grad_v = jnp.einsum("kgqt,qkgd->tkd", weights_b, cotangent, preferred_element_type=jnp.float32)
    grads = jnp.stack([grad_k, grad_v], 2)
    return (grad_q, grads.reshape(grads.shape[0], -1))


def split_halves(merged, head_index, level_bit):
    half_width = merged.shape[1] // 2
    lower_half = merged[:, :half_width]
    upper_half = merged[:, half_width:]
    upper_bit = head_index >> level_bit & 1
    kept_half = jnp.where(upper_bit == 1, upper_half, lower_half)
    sent_half = jnp.where(upper_bit == 1, lower_half, upper_half)
    return (kept_half, sent_half)


def general_device(query, key_value, grad_out, lengths, ancestors):
    col_width = key_value.shape[1]
    pair_width = 2 * HD
    rounds = (pair_width // col_width).bit_length() - 1 if col_width < pair_width else 0
    head_index = lax.axis_index("head")
    far_rows = (SEG_DEV - 1) * SLOT
    joined = key_value
    for level_bit in range(rounds):
        partner = from_partner(joined, "head", level_bit)
        upper_bit = head_index >> level_bit & 1
        joined = jnp.where(
            upper_bit == 1,
            jnp.concatenate([partner, joined], 1),
            jnp.concatenate([joined, partner], 1),
        )
    far_kv, far_lengths = (
        lax.all_gather(joined[:far_rows], "leaf", axis=0, tiled=True),
        lax.all_gather(lengths[: SEG_DEV - 1], "leaf", axis=0, tiled=True),
    )
    local_kv = joined.shape[1] // pair_width
    local_q = query.shape[1] // HD
    group_q = local_q // local_kv
    inv_root = HD ** (-0.5)
    positions = jnp.arange(SLOT)
    far_total = far_kv.shape[0]
    far_pieces = []
    far_starts = []
    own_parts = []
    grad_parts = []
    for slot_index in range(SEG_DEV):
        row_start = slot_index * SLOT
        row_valid = positions < lengths[slot_index]
        queries = query[row_start : row_start + SLOT].reshape(SLOT, local_kv, group_q, HD)
        cotangent = jnp.where(
            row_valid[:, None], grad_out[row_start : row_start + SLOT], jnp.zeros((), jnp.bfloat16)
        )
        cotangent = cotangent.reshape(SLOT, local_kv, group_q, HD)
        pieces = []
        key_masks = []
        slot_starts = []
        for level_index in range(slot_index):
            segment_id = ancestors[slot_index, level_index]
            block_index = segment_id // SEG_DEV * (SEG_DEV - 1) + segment_id % SEG_DEV
            block_start = block_index * SLOT
            pieces.append(lax.dynamic_slice_in_dim(far_kv, block_start, SLOT, 0))
            key_masks.append(
                jnp.broadcast_to(positions[None, :] < far_lengths[block_index], (SLOT, SLOT))
            )
            slot_starts.append(block_start)
        pieces.append(joined[row_start : row_start + SLOT])
        key_masks.append((positions[None, :] <= positions[:, None]) & row_valid[None, :])
        key_rows = jnp.concatenate(pieces, 0).reshape(-1, local_kv, 2, HD)
        grad_q, grad_kv = attend(
            queries, cotangent, key_rows, jnp.concatenate(key_masks, 1), inv_root
        )
        for level_index, block_start in enumerate(slot_starts):
            far_pieces.append(grad_kv[level_index * SLOT : (level_index + 1) * SLOT])
            far_starts.append(block_start)
        own_parts.append(grad_kv[slot_index * SLOT :])
        grad_parts.append(grad_q.reshape(SLOT, local_q * HD))
    far_grad = jnp.zeros((far_total, joined.shape[1]), jnp.float32)
    for piece, block_start in zip(far_pieces, far_starts):
        current = lax.dynamic_slice_in_dim(far_grad, block_start, SLOT, 0)
        far_grad = lax.dynamic_update_slice_in_dim(far_grad, current + piece, block_start, 0)
    merged = jnp.concatenate([far_grad] + own_parts, 0)
    for level_bit in reversed(range(rounds)):
        kept_half, sent_half = split_halves(merged, head_index, level_bit)
        merged = kept_half + from_partner(as_sent(sent_half), "head", level_bit).astype(
            sent_half.dtype
        )
    far_merged = merged[:far_total]
    own_sum = merged[far_total:]
    far_sum = lax.psum_scatter(
        far_merged.astype(jnp.bfloat16), "leaf", scatter_dimension=0, tiled=True
    ).astype(jnp.float32)
    combined = own_sum + jnp.concatenate([far_sum, jnp.zeros((SLOT, col_width), jnp.float32)], 0)
    return (jnp.concatenate(grad_parts, 0).astype(jnp.bfloat16), combined.astype(jnp.bfloat16))


FAR = SEG_DEV - 1
PAIRS = [(slot, level) for slot in range(SEG_DEV) for level in range(slot)]
F32 = jnp.float32
BF16 = jnp.bfloat16


def dot(left, right, left_dim, right_dim):
    return lax.dot_general(
        left, right, (((left_dim,), (right_dim,)), ((), ())), preferred_element_type=F32
    )


def kernel(n, kvh, group, lengths_in, ancestors_in, query, key_value, grad_out, dq_out, dkv_out, *scratch):
    scratch = list(scratch)
    lengths, ancestors, tree_in = scratch.pop(0), scratch.pop(0), scratch.pop(0)
    kv_buf = [[scratch.pop(0) for _ in range(FAR)] for _ in range(kvh)]
    last_kv, q_buf, do_buf, dq_buf, dkv_buf, lens, own, term, sent, arrived = scratch[:10]
    kv_in, last_in, q_in, do_in, dq_sem, dkv_sem, kv_send, kv_recv, len_send, len_recv, g_send, g_recv = scratch[10:]
    me = lax.axis_index("leaf")
    inv_root = HD ** (-0.5)
    width = 2 * HD
    cols = group * HD

    def kv_local(h, l):
        return pltpu.make_async_copy(
            key_value.at[pl.ds(l * SLOT, SLOT), pl.ds(h * width, width)], kv_buf[h][l].at[me], kv_in.at[h, l]
        )

    def last_local(h):
        return pltpu.make_async_copy(
            key_value.at[pl.ds(FAR * SLOT, SLOT), pl.ds(h * width, width)], last_kv.at[h], last_in.at[h]
        )

    def rows_in(source, target, sem, j):
        rows = pl.ds(j * SLOT, SLOT)
        return pltpu.make_async_copy(source.at[rows], target.at[rows], sem.at[j])

    tree = [
        pltpu.make_async_copy(lengths_in, lengths, tree_in.at[0]),
        pltpu.make_async_copy(ancestors_in, ancestors, tree_in.at[1]),
    ]
    for copy in tree:
        copy.start()
    for h in range(kvh):
        for l in range(FAR):
            kv_local(h, l).start()
    for h in range(kvh):
        last_local(h).start()
    for j in range(SEG_DEV):
        rows_in(query, q_buf, q_in, j).start()
        rows_in(grad_out, do_buf, do_in, j).start()

    barrier = pltpu.get_barrier_semaphore()
    for k in range(1, n):
        pl.semaphore_signal(
            barrier, inc=1, device_id={"leaf": lax.rem(me + k, n)}, device_id_type=pl.DeviceIdType.MESH
        )
    for copy in tree:
        copy.wait()
    for l in range(FAR):
        lens[me, l] = jnp.full((128,), lengths[l], jnp.int32)
    pl.semaphore_wait(barrier, n - 1)

    def lens_copy(k):
        return pltpu.make_async_remote_copy(
            src_ref=lens.at[me],
            dst_ref=lens.at[me],
            send_sem=len_send.at[k - 1],
            recv_sem=len_recv.at[k - 1],
            device_id={"leaf": lax.rem(me + k, n)},
            device_id_type=pl.DeviceIdType.MESH,
        )

    def hop_ok(way, s):
        if way == 0:
            return (me < n - 1) & (me - s >= 0)
        return (me > 0) & (me + s <= n - 1)

    def got_ok(way, s):
        return me - 1 - s >= 0 if way == 0 else me + 1 + s <= n - 1

    def kv_copy(way, s, h, l, block):
        ref = kv_buf[h][l].at[block]
        return pltpu.make_async_remote_copy(
            src_ref=ref,
            dst_ref=ref,
            send_sem=kv_send.at[way, s, h, l],
            recv_sem=kv_recv.at[way, s, h, l],
            device_id={"leaf": me + 1 if way == 0 else me - 1},
            device_id_type=pl.DeviceIdType.MESH,
        )

    def kv_start(way, s, h, l):
        @pl.when(hop_ok(way, s))
        def _():
            kv_copy(way, s, h, l, me - s if way == 0 else me + s).start()

    def kv_arrive(way, s, h, l):
        @pl.when(got_ok(way, s))
        def _():
            kv_copy(way, s, h, l, me - 1 - s if way == 0 else me + 1 + s).wait_recv()

    def own_sends(h, sends):
        if h == kvh:
            return
        for way in (0, 1):
            before = me if way == 0 else n - 1 - me

            @pl.when((before == sends) & hop_ok(way, 0))
            def _():
                for l in range(FAR):
                    kv_copy(way, 0, h, l, me).start()

    def hop(h, s):
        for l in range(FAR):
            for way in (0, 1):
                kv_arrive(way, s, h, l)
                if s + 1 < n - 1:
                    kv_start(way, s + 1, h, l)
        own_sends(h + 1, s + 1)

    key_pos = lax.broadcasted_iota(jnp.int32, (SLOT, 128), 0)
    query_pos = lax.broadcasted_iota(jnp.int32, (SLOT, 128), 1) & (SLOT - 1)
    parts = 2 if group % 4 == 0 else 1
    heads = group // parts
    lanes = heads * SLOT

    def wide(tile):
        return jnp.concatenate([tile] * (lanes // 128), 1)

    def home(j, l):
        return lax.div(ancestors[l, j], SEG_DEV)

    def dq_copy(h, j):
        view = (pl.ds(j * SLOT, SLOT), pl.ds(h * cols, cols))
        return pltpu.make_async_copy(dq_buf.at[view], dq_out.at[view], dq_sem.at[h, j])

    def compute(h, j):
        rows = pl.ds(j * SLOT, SLOT)
        pieces, biases = [], []
        for l in range(j):
            place = home(j, l)
            pieces.append(kv_buf[h][l][place])
            biases.append(jnp.where(key_pos < lens[place, l : l + 1, :], 0.0, masked_score))
        pieces.append(kv_buf[h][j][me] if j < FAR else last_kv[h])
        biases.append(
            jnp.where((key_pos < lengths[j]) & (key_pos <= query_pos), 0.0, masked_score)
        )
        keys = jnp.concatenate([piece[:, :HD] for piece in pieces], 0)
        values = jnp.concatenate([piece[:, HD:] for piece in pieces], 0)
        bias = wide(jnp.concatenate(biases, 0))
        valid = jnp.where(key_pos < lengths[j], 1.0, 0.0).astype(BF16)
        grad_k = grad_v = None
        for part in range(parts):
            at = [(h * group + part * heads + g) * HD for g in range(heads)]
            q = jnp.concatenate([q_buf[rows, pl.ds(a, HD)] for a in at], 0)
            do = jnp.concatenate([do_buf[rows, pl.ds(a, HD)] * valid for a in at], 0)
            scores = dot(keys, q, 1, 1) * (inv_root * math.log2(math.e)) + bias
            top = jnp.max(scores, 0, keepdims=True)
            powers = jnp.exp2(scores - top)
            probs = powers * (1.0 / jnp.sum(powers, 0, keepdims=True))
            probs_b = probs.astype(BF16)
            dprobs = dot(values, do, 1, 1)
            delta = jnp.sum(probs_b.astype(F32) * dprobs, 0, keepdims=True)
            dscores = (probs * (dprobs - delta)).astype(BF16)
            part_v = dot(probs_b, do, 1, 0)
            part_k = dot(dscores, q, 1, 0)
            grad_v = part_v if grad_v is None else grad_v + part_v
            grad_k = part_k if grad_k is None else grad_k + part_k
            grad_q = (dot(dscores, keys, 0, 0) * inv_root).astype(BF16)
            for g, a in enumerate(at):
                dq_buf[rows, pl.ds(a, HD)] = grad_q[g * SLOT : (g + 1) * SLOT]
        dq_copy(h, j).start()
        grads = jnp.concatenate([grad_k * inv_root, grad_v], 1)
        for l in range(j):
            term[h, PAIRS.index((j, l))] = grads[l * SLOT : (l + 1) * SLOT]
        own[h, j] = grads[j * SLOT :]

    def local_terms(h, l, target):
        total = None
        for j in range(l + 1, SEG_DEV):
            weight = jnp.where(home(j, l) == target, 1.0, 0.0).astype(F32)
            one = term[h, PAIRS.index((j, l))] * weight
            total = one if total is None else total + one
        return total

    def g_copy(way, k, h, l, target):
        return pltpu.make_async_remote_copy(
            src_ref=sent.at[h, target, l],
            dst_ref=arrived.at[way, h, target, l],
            send_sem=g_send.at[way, k - 1, h, l],
            recv_sem=g_recv.at[way, k - 1, h, l],
            device_id={"leaf": me + 1 if way == 0 else me - 1},
            device_id_type=pl.DeviceIdType.MESH,
        )

    def g_target(way, k):
        return me + k if way == 0 else me - k

    def g_ok(way, k):
        return me + k <= n - 1 if way == 0 else me - k >= 0

    def g_behind(way):
        return me > 0 if way == 0 else me < n - 1

    def lead_terms(h, l):
        for way in (0, 1):
            @pl.when(me == (0 if way == 0 else n - 1))
            def _():
                for k in range(n - 1, 0, -1):
                    target = g_target(way, k)
                    sent[h, target, l] = local_terms(h, l, target).astype(BF16)
                    g_copy(way, k, h, l, target).start()

    def relay_terms(h, k, l):
        for way in (0, 1):
            @pl.when(g_ok(way, k) & g_behind(way))
            def _():
                target = g_target(way, k)
                g_copy(way, k + 1, h, l, target).wait_recv()
                total = local_terms(h, l, target).astype(BF16).astype(F32)
                total = total + arrived[way, h, target, l].astype(F32)
                sent[h, target, l] = total.astype(BF16)
                g_copy(way, k, h, l, target).start()

    def dkv_copy(h, j):
        view = (pl.ds(j * SLOT, SLOT), pl.ds(h * width, width))
        return pltpu.make_async_copy(dkv_buf.at[view], dkv_out.at[view], dkv_sem.at[h, j])

    def finish_last(h):
        dkv_buf[pl.ds(FAR * SLOT, SLOT), pl.ds(h * width, width)] = own[h, FAR].astype(BF16)
        dkv_copy(h, FAR).start()

    def finish(h, l):
        own[h, l] = own[h, l] + local_terms(h, l, me).astype(BF16).astype(F32)
        for way in (0, 1):
            @pl.when(g_behind(way))
            def _():
                g_copy(way, 1, h, l, me).wait_recv()
                own[h, l] = own[h, l] + arrived[way, h, me, l].astype(F32)
        dkv_buf[pl.ds(l * SLOT, SLOT), pl.ds(h * width, width)] = own[h, l].astype(BF16)
        dkv_copy(h, l).start()

    for k in range(1, n):
        lens_copy(k).start()
    for l in range(FAR):
        kv_local(0, l).wait()
        kv_start(0, 0, 0, l)
        kv_start(1, 0, 0, l)
    for h in range(1, kvh):
        for l in range(FAR):
            kv_local(h, l).wait()
    own_sends(1, 0)
    for h in range(kvh):
        last_local(h).wait()
    for k in range(1, n):
        lens_copy(k).wait()
    for j in range(SEG_DEV):
        rows_in(query, q_buf, q_in, j).wait()
        rows_in(grad_out, do_buf, do_in, j).wait()

    for h in range(kvh):
        compute(h, 0)
    for s in range(n - 1):
        hop(0, s)

    order = [(h, j) for h in range(kvh) for j in range(FAR, 0, -1)]
    for step in range(len(order) + n):
        if step < len(order):
            h, j = order[step]
            compute(h, j)
            lead_terms(h, j - 1)
            if h + 1 < kvh and FAR - j < n - 2:
                hop(h + 1, FAR - j)
        for k in range(n - 2, 0, -1):
            behind = step - (n - 1 - k)
            if 0 <= behind < len(order):
                done_h, done_j = order[behind]
                relay_terms(done_h, k, done_j - 1)
        behind = step - n
        if 0 <= behind < len(order):
            done_h, done_j = order[behind]
            finish(done_h, done_j - 1)
        if step < len(order):
            h, j = order[step]
            if j == 1:
                finish_last(h)
                for s in range(n - 2 if FAR > n - 2 else FAR, n - 1):
                    if h + 1 < kvh:
                        hop(h + 1, s)

    for k in range(1, n):
        for way in (0, 1):
            @pl.when(g_ok(way, k))
            def _():
                for h in range(kvh):
                    for l in range(FAR):
                        g_copy(way, k, h, l, g_target(way, k)).wait_send()
    for s in range(n - 1):
        for way in (0, 1):
            @pl.when(hop_ok(way, s))
            def _():
                for h in range(kvh):
                    for l in range(FAR):
                        kv_copy(way, s, h, l, me - s if way == 0 else me + s).wait_send()
    for h in range(kvh):
        for j in range(SEG_DEV):
            dq_copy(h, j).wait()
            dkv_copy(h, j).wait()


def line_device(query, key_value, grad_out, lengths, ancestors):
    n = lax.axis_size("leaf")
    width = 2 * HD
    kvh = key_value.shape[1] // width
    group = query.shape[1] // (kvh * HD)
    tile = (SLOT, width)
    dma = pltpu.SemaphoreType.DMA
    scratch = [
        pltpu.SMEM(lengths.shape, jnp.int32),
        pltpu.SMEM(ancestors.shape[::-1], jnp.int32),
        dma((2,)),
    ]
    scratch += [pltpu.VMEM((n,) + tile, BF16) for _ in range(kvh * FAR)]
    scratch += [
        pltpu.VMEM((kvh,) + tile, BF16),
        pltpu.VMEM(query.shape, BF16),
        pltpu.VMEM(query.shape, BF16),
        pltpu.VMEM(query.shape, BF16),
        pltpu.VMEM(key_value.shape, BF16),
        pltpu.VMEM((n, 8, 128), jnp.int32),
        pltpu.VMEM((kvh, SEG_DEV) + tile, F32),
        pltpu.VMEM((kvh, len(PAIRS)) + tile, F32),
        pltpu.VMEM((kvh, n, FAR) + tile, BF16),
        pltpu.VMEM((2, kvh, n, FAR) + tile, BF16),
    ]
    scratch += [dma((kvh, FAR)), dma((kvh,)), dma((SEG_DEV,)), dma((SEG_DEV,))]
    scratch += [dma((kvh, SEG_DEV)), dma((kvh, SEG_DEV))]
    scratch += [dma((2, n - 1, kvh, FAR)), dma((2, n - 1, kvh, FAR)), dma((n - 1,)), dma((n - 1,))]
    scratch += [dma((2, n - 1, kvh, FAR)), dma((2, n - 1, kvh, FAR))]
    anywhere = pl.BlockSpec(memory_space=pl.ANY)
    return pl.pallas_call(
        functools.partial(kernel, n, kvh, group),
        out_shape=(
            jax.ShapeDtypeStruct(query.shape, BF16),
            jax.ShapeDtypeStruct(key_value.shape, BF16),
        ),
        in_specs=[anywhere] * 5,
        out_specs=(anywhere, anywhere),
        scratch_shapes=scratch,
        compiler_params=pltpu.CompilerParams(
            collective_id=0, has_side_effects=True, vmem_limit_bytes=60 * 1024 * 1024
        ),
    )(lengths, ancestors.T, query, key_value, grad_out)


def on_device(query, key_value, grad_out, lengths, ancestors):
    whole_heads = key_value.shape[1] % (2 * HD) == 0
    step = line_device if whole_heads else general_device
    return step(query, key_value, grad_out, lengths, ancestors)


def solution(mesh):
    return jax.shard_map(
        on_device,
        mesh=mesh,
        in_specs=(
            P(("grp", "leaf"), "head"),
            P(("grp", "leaf"), "head"),
            P(("grp", "leaf"), "head"),
            P(("grp", "leaf")),
            P(("grp", "leaf"), None),
        ),
        out_specs=(P(("grp", "leaf"), "head"), P(("grp", "leaf"), "head")),
        check_vma=False,
    )
```
